32 devices in a mesh: gx: 8 (over z, core), gy: 4 (over y, x).
Axes of the slice: x: 2, y: 2, z: 4, core: 2. Of those that a mesh axis runs over, the one named last changes fastest.
Arguments:
- density: float32 [64, 128, 256], P('gx', 'gy'), may hold values from 0.5 to 2
- energy: float32 [64, 128, 256], P('gx', 'gy'), may hold values from 0.5 to 2
- velocity_x: float32 [64, 128, 256], P('gx', 'gy'), may hold values from -0.5 to 0.5
- velocity_y: float32 [64, 128, 256], P('gx', 'gy'), may hold values from -0.5 to 0.5
- velocity_z: float32 [64, 128, 256], P('gx', 'gy'), may hold values from -0.5 to 0.5
- time_step: float32 [1], replicated, may hold values from 0.1 to 0.2
Outputs:
- new_density: float32 [64, 128, 256], P('gx', 'gy')
- new_energy: float32 [64, 128, 256], P('gx', 'gy')
- new_velocity_x: float32 [64, 128, 256], P('gx', 'gy')
- new_velocity_y: float32 [64, 128, 256], P('gx', 'gy')
- new_velocity_z: float32 [64, 128, 256], P('gx', 'gy')
- next_step: float32 [1], replicated
The draws below stay inside these ranges and needn't reach their ends.
All inputs are finite; a program needn't handle non-finite values.
Results may differ from the reference program's by a relative error of at most 0.0003.
Values sent between devices are 32-bit elements; how exact they have to be, the bound alone decides.
A program may use at most 64 MiB of HBM per device.

```python
import math
import jax
import jax.numpy as jnp

NZ = 256
NX = 64
NY = 128


def level_of(own_key, shape, pieces, smallest, high):
    def one(position, parts):
        draws = jax.random.uniform(jax.random.fold_in(jax.random.fold_in(own_key, 6), position), (parts,), jnp.float32, smallest / len(pieces), high / len(pieces))
        return jnp.repeat(jnp.exp(draws), shape[position] // parts).reshape((-1,) + (1,) * (len(shape) - position - 1))

    factor_of = one(*pieces[0])
    for cut in pieces[1:]:
        factor_of = factor_of * one(*cut)
    return factor_of


def setup_inputs(seed: int = 0) -> dict:
    splits = jax.random.split(jax.random.key(seed), 7)
    return {
        "density": jnp.clip(jnp.exp(math.log(2.0) - 1.3862944 * jax.random.uniform(splits[0], (NX, NY, NZ), jnp.float32) ** level_of(splits[0], (NX, NY, NZ), ((0, 8), (1, 4)), -0.2, 0.2)), 0.5, 2.0),
        "energy": jnp.clip(jnp.exp(math.log(2.0) - 1.3862944 * jax.random.uniform(splits[1], (NX, NY, NZ), jnp.float32) ** level_of(splits[1], (NX, NY, NZ), ((0, 8), (1, 4)), -0.2, 0.2)), 0.5, 2.0),
        "velocity_x": jnp.clip(jax.random.uniform(splits[2], (NX, NY, NZ), jnp.float32, -0.5, 0.5) * level_of(splits[2], (NX, NY, NZ), ((0, 8), (1, 4)), -0.4, 0.0), -0.5, 0.5),
        "velocity_y": jnp.clip(jax.random.uniform(splits[3], (NX, NY, NZ), jnp.float32, -0.5, 0.5) * level_of(splits[3], (NX, NY, NZ), ((0, 8), (1, 4)), -0.4, 0.0), -0.5, 0.5),
        "velocity_z": jnp.clip(jax.random.uniform(splits[4], (NX, NY, NZ), jnp.float32, -0.5, 0.5) * level_of(splits[4], (NX, NY, NZ), ((0, 8), (1, 4)), -0.4, 0.0), -0.5, 0.5),
        "time_step": jnp.clip(jax.random.uniform(splits[5], (1,), jnp.float32, 0.1, 0.2), 0.1, 0.2),
    }


def shifted(field, offset, along):
    return jnp.roll(field, -offset, along)

def central(field, along):
    return 0.5 * (shifted(field, 1, along) - shifted(field, -1, along))

def van_leer(left_diff, right_diff):
    product = left_diff * right_diff
    agree = product > 0
    return jnp.where(agree, 2.0 * product / jnp.where(agree, left_diff + right_diff, 1.0), 0.0)

def sweep_roll(density, mass_energy, velocity, delta_t, along):
    courant = delta_t * (0.5 * (velocity + shifted(velocity, 1, along)))
    weight = 0.5 * (1.0 - jnp.abs(courant))

    def face_value(field):
        slope = van_leer(field - shifted(field, -1, along), shifted(field, 1, along) - field)
        ahead = field + weight * slope
        behind = shifted(field, 1, along) - weight * shifted(slope, 1, along)
        return jnp.where(courant > 0, ahead, behind)
    flux = courant * face_value(density)
    energy_flux = courant * face_value(mass_energy)
    dens_out = density + shifted(flux, -1, along) - flux
    mass_out = mass_energy + shifted(energy_flux, -1, along) - energy_flux
    return (dens_out, mass_out)

def reference(density, energy, velocity_x, velocity_y, velocity_z, time_step):
    delta_t = time_step[0]
    pressure = 0.4 * density * energy
    diverge = central(velocity_x, 0) + central(velocity_y, 1) + central(velocity_z, 2)
    volume = 1.0 + delta_t * diverge
    lag_density = density / volume
    energy_half = energy - 0.5 * delta_t * pressure * diverge / density
    press_half = 0.4 * density * energy_half
    lag_energy = energy - delta_t * press_half * diverge / density
    new_velx = velocity_x - delta_t * central(pressure, 0) / density
    new_vely = velocity_y - delta_t * central(pressure, 1) / density
    new_velz = velocity_z - delta_t * central(pressure, 2) / density
    mass_energy = lag_density * lag_energy
    dens_a, mass_a = sweep_roll(lag_density, mass_energy, new_velx, delta_t, 0)
    dens_b, mass_b = sweep_roll(dens_a, mass_a, new_vely, delta_t, 1)
    dens_c, mass_c = sweep_roll(dens_b, mass_b, new_velz, delta_t, 2)
    new_energy = mass_c / dens_c
    speed = jnp.sqrt(0.56 * new_energy) + jnp.abs(new_velx) + jnp.abs(new_vely) + jnp.abs(new_velz)
    limit = jnp.min(0.5 / speed).reshape(1)
    return (dens_c, new_energy, new_velx, new_vely, new_velz, limit)
```

```python
import functools

import jax
import jax.numpy as jnp
from jax import lax
from jax.experimental import pallas as pl
from jax.experimental.pallas import tpu as pltpu
from jax.sharding import PartitionSpec as P

MESH = pl.DeviceIdType.MESH


def limited(left, right):
    product = left * right
    agree = product > 0
    return jnp.where(agree, 2.0 * product / jnp.where(agree, left + right, 1.0), 0.0)


def kernel(
    nx, ny,
    t_ref, d_hbm, e_hbm, vx_hbm, vy_hbm, vz_hbm,
    dens_out, energy_out, nvx_out, nvy_out, nvz_out, limit_out,
    d_s, e_s, xp, vy_s, vz_s, div_s, rate_s,
    a_send, a_lo, a_hi, lm, nvx_h, swept, c_send, c_lo, c_hi,
    top_s, top_x, top_y,
    load_sem, send_sem, recv_sem, x_send, x_recv, y_send, y_recv,
):
    layers, rows, cols = d_s.shape
    ix, iy = lax.axis_index("gx"), lax.axis_index("gy")

    def along_x(step):
        return (lax.rem(ix + step, nx), iy)

    def along_y(step):
        return (ix, lax.rem(iy + step, ny))

    barrier = pltpu.get_barrier_semaphore()
    for step in range(1, nx):
        pl.semaphore_signal(barrier, inc=1, device_id=along_x(step), device_id_type=MESH)
    for step in range(1, ny):
        pl.semaphore_signal(barrier, inc=1, device_id=along_y(step), device_id_type=MESH)

    loads = [
        pltpu.make_async_copy(d_hbm, d_s, load_sem.at[0]),
        pltpu.make_async_copy(e_hbm, e_s, load_sem.at[1]),
        pltpu.make_async_copy(vx_hbm, xp.at[pl.ds(1, layers), 0], load_sem.at[2]),
        pltpu.make_async_copy(vy_hbm, vy_s, load_sem.at[3]),
        pltpu.make_async_copy(vz_hbm, vz_s, load_sem.at[4]),
    ]
    for load in loads:
        load.start()
    t = t_ref[0]

    def remote(src, dst, index, device):
        return pltpu.make_async_remote_copy(
            src_ref=src, dst_ref=dst, send_sem=send_sem.at[index], recv_sem=recv_sem.at[index],
            device_id=device, device_id_type=MESH,
        )

    x_next, x_prev = along_x(1), along_x(nx - 1)
    y_next, y_prev = along_y(1), along_y(ny - 1)

    for load in loads:
        load.wait()

    @pl.loop(0, layers)
    def _(l):
        xp[l + 1, 1] = 0.4 * d_s[l] * e_s[l]

    a_send[0, 0] = vy_s[:, 0, :]
    a_send[0, 1] = xp[1 : layers + 1, 1, 0, :]
    a_send[1, 0] = vy_s[:, rows - 1, :]
    a_send[1, 1] = xp[1 : layers + 1, 1, rows - 1, :]

    pl.semaphore_wait(barrier, nx - 1 + ny - 1)
    first = [
        remote(xp.at[1], xp.at[layers + 1], 0, x_prev),
        remote(xp.at[layers], xp.at[0], 1, x_next),
        remote(a_send.at[0], a_hi, 2, y_prev),
        remote(a_send.at[1], a_lo, 3, y_next),
    ]
    for copy in first:
        copy.start()

    @pl.loop(0, layers)
    def _(l):
        rate = (0.5 * t) / d_s[l]
        vz, p = vz_s[l], xp[l + 1, 1]
        rate_s[l] = rate
        div_s[l] = 0.5 * (pltpu.roll(vz, cols - 1, 1) - pltpu.roll(vz, 1, 1))
        nvz_out[l] = vz - rate * (pltpu.roll(p, cols - 1, 1) - pltpu.roll(p, 1, 1))

    for copy in first:
        copy.wait()

    row = lax.broadcasted_iota(jnp.int32, (rows, cols), 0)

    def lagrange(l):
        def diff_y(f, which):
            ahead = jnp.where(row == rows - 1, a_hi[which, pl.ds(l, 1), :], pltpu.roll(f, rows - 1, 0))
            behind = jnp.where(row == 0, a_lo[which, pl.ds(l, 1), :], pltpu.roll(f, 1, 0))
            return ahead - behind

        rate, vy, energy = rate_s[l], vy_s[l], e_s[l]
        diverge = 0.5 * (xp[l + 2, 0] - xp[l, 0]) + 0.5 * diff_y(vy, 0) + div_s[l]
        td = t * diverge
        half = energy - 0.2 * td * energy
        lag_energy = energy - 0.4 * td * half
        lag_density = d_s[l] / (1.0 + td)
        lm[l + 2, 0] = lag_density
        lm[l + 2, 1] = lag_density * lag_energy
        nvx = xp[l + 1, 0] - rate * (xp[l + 2, 1] - xp[l, 1])
        nvx_h[l + 1] = nvx
        nvx_out[l] = nvx
        nvy_out[l] = vy - rate * diff_y(xp[l + 1, 1], 1)

    @pl.loop(0, 4)
    def _(i):
        lagrange(i + (i // 2) * (layers - 4))

    second = [
        remote(lm.at[pl.ds(2, 2)], lm.at[pl.ds(layers + 2, 2)], 4, x_prev),
        remote(lm.at[pl.ds(layers, 2)], lm.at[pl.ds(0, 2)], 5, x_next),
        remote(nvx_h.at[1], nvx_h.at[layers + 1], 6, x_prev),
        remote(nvx_h.at[layers], nvx_h.at[0], 7, x_next),
    ]
    for copy in second:
        copy.start()

    @pl.loop(2, layers - 2)
    def _(l):
        lagrange(l)

    def sweep_x(lower, upper):
        @pl.loop(0, rows // 8)
        def _(block):
            part = pl.ds(pl.multiple_of(block * 8, 8), 8)

            def slope(f, l):
                return limited(f[l] - f[l - 1], f[l + 1] - f[l])

            courants = {}
            for l in range(lower - 1, upper):
                courants[l] = (0.5 * t) * (nvx_h[l + 1, part] + nvx_h[l + 2, part])
            for field in range(2):
                f = {l: lm[l + 2, field, part] for l in range(lower - 2, upper + 2)}
                here = slope(f, lower - 1)
                flux = None
                for l in range(lower - 1, upper):
                    courant = courants[l]
                    weight = 0.5 - 0.5 * jnp.abs(courant)
                    after = slope(f, l + 1)
                    face = jnp.where(courant > 0, f[l] + weight * here, f[l + 1] - weight * after)
                    now = courant * face
                    if flux is not None:
                        swept[l, field, part] = f[l] + flux - now
                    flux, here = now, after

    if layers > 4:
        sweep_x(2, layers - 2)
    for copy in second:
        copy.wait()
    sweep_x(0, 2)
    sweep_x(layers - 2, layers)

    for side, edge in enumerate((0, rows - 2)):
        for j in range(2):
            for field in range(2):
                c_send[side, 2 * field + j] = swept[:, field, edge + j, :]
        c_send[side, 4] = nvy_out[:, 0 if side == 0 else rows - 1, :]

    third = [
        remote(c_send.at[0], c_hi, 8, y_prev),
        remote(c_send.at[1], c_lo, 9, y_next),
    ]
    for copy in third:
        copy.start()
    for copy in third:
        copy.wait()

    tall = rows + 8
    tile = lax.broadcasted_iota(jnp.int32, (8, cols), 0)

    def sweep(fields, velocity, axis):
        size = velocity.shape[axis]

        def ahead(f):
            return pltpu.roll(f, size - 1, axis)

        def behind(f):
            return pltpu.roll(f, 1, axis)

        courant = (0.5 * t) * (velocity + ahead(velocity))
        weight = 0.5 - 0.5 * jnp.abs(courant)
        out = []
        for f in fields:
            after = ahead(f)
            right = after - f
            slope = limited(behind(right), right)
            flux = courant * jnp.where(courant > 0, f + weight * slope, after - weight * ahead(slope))
            out.append(f + behind(flux) - flux)
        return out

    def finish(l, top):
        def halo(low_first, low_last, high_first, high_last):
            low = jnp.where(tile == 7, c_lo[low_last, pl.ds(l, 1), :], c_lo[low_first, pl.ds(l, 1), :])
            high = jnp.where(tile == 0, c_hi[high_first, pl.ds(l, 1), :], c_hi[high_last, pl.ds(l, 1), :])
            return jnp.where(tile < 4, high, low)

        fields = [
            jnp.concatenate([swept[l, k], halo(2 * k, 2 * k + 1, 2 * k, 2 * k + 1)], axis=0)
            for k in range(2)
        ]
        nvy = nvy_out[l]
        velocity = jnp.concatenate([nvy, halo(4, 4, 4, 4)], axis=0)
        fields = [f[:rows] for f in sweep(fields, velocity, 0)]
        nvz = nvz_out[l]
        density, mass = sweep(fields, nvz, 1)
        energy = mass / density
        dens_out[l] = density
        energy_out[l] = energy
        speed = jnp.sqrt(0.56 * energy) + jnp.abs(nvx_out[l]) + jnp.abs(nvy) + jnp.abs(nvz)
        return jnp.maximum(top, speed)

    top = lax.fori_loop(0, layers, finish, jnp.zeros((rows, cols), jnp.float32))

    def reduced(value):
        return jnp.full((8, 128), jnp.max(value), jnp.float32)

    def share(value, slot, buffer, count, device, sends, recvs):
        top_s[slot] = value
        copies = [
            pltpu.make_async_remote_copy(
                src_ref=top_s.at[slot], dst_ref=buffer.at[step - 1],
                send_sem=sends.at[step - 1], recv_sem=recvs.at[step - 1],
                device_id=device(step), device_id_type=MESH,
            )
            for step in range(1, count)
        ]
        for copy in copies:
            copy.start()
        for copy in copies:
            copy.wait()
        for step in range(1, count):
            value = jnp.maximum(value, buffer[step - 1])
        return value

    best = share(reduced(top), 0, top_x, nx, along_x, x_send, x_recv)
    best = share(best, 1, top_y, ny, along_y, y_send, y_recv)
    limit_out[0] = jnp.max(0.5 / best)


def local(nx, ny, density, energy, velocity_x, velocity_y, velocity_z, time_step):
    layers, rows, cols = density.shape
    full = jax.ShapeDtypeStruct(density.shape, jnp.float32)

    def vmem(*shape):
        return pltpu.VMEM(shape, jnp.float32)

    dma = pltpu.SemaphoreType.DMA
    return pl.pallas_call(
        functools.partial(kernel, nx, ny),
        out_shape=(full,) * 5 + (jax.ShapeDtypeStruct((1,), jnp.float32),),
        in_specs=[pl.BlockSpec(memory_space=pltpu.SMEM)] + [pl.BlockSpec(memory_space=pl.ANY)] * 5,
        out_specs=(pl.BlockSpec(memory_space=pltpu.VMEM),) * 5 + (pl.BlockSpec(memory_space=pltpu.SMEM),),
        scratch_shapes=[
            vmem(layers, rows, cols), vmem(layers, rows, cols),
            vmem(layers + 2, 2, rows, cols),
            vmem(layers, rows, cols), vmem(layers, rows, cols),
            vmem(layers, rows, cols), vmem(layers, rows, cols),
            vmem(2, 2, layers, cols), vmem(2, layers, cols), vmem(2, layers, cols),
            vmem(layers + 4, 2, rows, cols),
            vmem(layers + 2, rows, cols),
            vmem(layers, 2, rows, cols),
            vmem(2, 5, layers, cols), vmem(5, layers, cols), vmem(5, layers, cols),
            vmem(2, 8, 128), vmem(nx - 1, 8, 128), vmem(ny - 1, 8, 128),
            dma((5,)), dma((10,)), dma((10,)),
            dma((nx - 1,)), dma((nx - 1,)), dma((ny - 1,)), dma((ny - 1,)),
        ],
        compiler_params=pltpu.CompilerParams(
            collective_id=0, has_side_effects=True, vmem_limit_bytes=32 * 1024 * 1024
        ),
    )(time_step, density, energy, velocity_x, velocity_y, velocity_z)


def solution(mesh):
    block = P("gx", "gy", None)
    return jax.shard_map(
        functools.partial(local, mesh.shape["gx"], mesh.shape["gy"]),
        mesh=mesh,
        in_specs=(block,) * 5 + (P(),),
        out_specs=(block,) * 5 + (P(),),
        check_vma=False,
    )
```

```python
import functools

import jax
import jax.numpy as jnp
from jax import lax
from jax.experimental import pallas as pl
from jax.experimental.pallas import tpu as pltpu
from jax.sharding import PartitionSpec as P

MESH = pl.DeviceIdType.MESH


def inverse(value):
    guess = pl.reciprocal(value, approx=True)
    return guess * (2.0 - value * guess)


def limited(left, right):
    product = left * right
    return jnp.maximum(product, 0.0) * inverse(jnp.where(product > 0, left + right, 1.0))


def upwind(courant):
    positive = courant > 0
    return positive, jnp.where(positive, 1.0, -1.0) - courant


def store(*refs):
    sources, targets, sem = refs[:5], refs[5:10], refs[10]
    copies = [
        pltpu.make_async_copy(source, target, sem.at[k])
        for k, (source, target) in enumerate(zip(sources, targets))
    ]
    for copy in copies:
        copy.start()
    for copy in copies:
        copy.wait()


def kernel(
    nx, ny,
    t_ref, d_hbm, e_hbm, vx_hbm, vy_hbm, vz_hbm,
    dens_out, energy_out, nvx_out, nvy_out, nvz_out, limit_out,
    d_s, e_s, xp, vy_s, vz_s, div_s, rate_s,
    a_send, a_lo, a_hi, lm, nvx_h, swept, m_send, m_lo, m_hi, o_send, o_lo, o_hi,
    top_s, top_x, top_y,
    load_sem, send_sem, recv_sem, x_send, x_recv, y_send, y_recv,
):
    layers, rows, cols = d_s.shape
    ix, iy = lax.axis_index("gx"), lax.axis_index("gy")

    def along_x(step):
        return (lax.rem(ix + step, nx), iy)

    def along_y(step):
        return (ix, lax.rem(iy + step, ny))

    barrier = pltpu.get_barrier_semaphore()
    for step in range(1, nx):
        pl.semaphore_signal(barrier, inc=1, device_id=along_x(step), device_id_type=MESH)
    for step in range(1, ny):
        pl.semaphore_signal(barrier, inc=1, device_id=along_y(step), device_id_type=MESH)

    loads = [
        pltpu.make_async_copy(d_hbm, d_s, load_sem.at[0]),
        pltpu.make_async_copy(e_hbm, e_s, load_sem.at[1]),
        pltpu.make_async_copy(vx_hbm, xp.at[pl.ds(1, layers), 0], load_sem.at[2]),
        pltpu.make_async_copy(vy_hbm, vy_s, load_sem.at[3]),
        pltpu.make_async_copy(vz_hbm, vz_s, load_sem.at[4]),
    ]
    for load in loads:
        load.start()
    t = t_ref[0]

    def remote(src, dst, index, device):
        return pltpu.make_async_remote_copy(
            src_ref=src, dst_ref=dst, send_sem=send_sem.at[index], recv_sem=recv_sem.at[index],
            device_id=device, device_id_type=MESH,
        )

    x_next, x_prev = along_x(1), along_x(nx - 1)
    y_next, y_prev = along_y(1), along_y(ny - 1)

    for load in loads:
        load.wait()

    @pl.loop(0, layers)
    def _(l):
        xp[l + 1, 1] = 0.4 * d_s[l] * e_s[l]

    a_send[0, 0] = vy_s[:, 0, :]
    a_send[0, 1] = xp[1 : layers + 1, 1, 0, :]
    a_send[1, 0] = vy_s[:, rows - 1, :]
    a_send[1, 1] = xp[1 : layers + 1, 1, rows - 1, :]

    pl.semaphore_wait(barrier, nx - 1 + ny - 1)
    first = [
        remote(xp.at[1], xp.at[layers + 1], 0, x_prev),
        remote(xp.at[layers], xp.at[0], 1, x_next),
        remote(a_send.at[0], a_hi, 2, y_prev),
        remote(a_send.at[1], a_lo, 3, y_next),
    ]
    for copy in first:
        copy.start()

    @pl.loop(0, layers)
    def _(l):
        rate = (0.5 * t) * inverse(d_s[l])
        vz, p = vz_s[l], xp[l + 1, 1]
        rate_s[l] = rate
        div_s[l] = 0.5 * (pltpu.roll(vz, cols - 1, 1) - pltpu.roll(vz, 1, 1))
        nvz_out[l] = vz - rate * (pltpu.roll(p, cols - 1, 1) - pltpu.roll(p, 1, 1))

    for copy in first:
        copy.wait()

    row = lax.broadcasted_iota(jnp.int32, (rows, cols), 0)

    def lagrange(l):
        def diff_y(f, which):
            ahead = jnp.where(row == rows - 1, a_hi[which, pl.ds(l, 1), :], pltpu.roll(f, rows - 1, 0))
            behind = jnp.where(row == 0, a_lo[which, pl.ds(l, 1), :], pltpu.roll(f, 1, 0))
            return ahead - behind

        rate, vy, energy = rate_s[l], vy_s[l], e_s[l]
        diverge = 0.5 * (xp[l + 2, 0] - xp[l, 0]) + 0.5 * diff_y(vy, 0) + div_s[l]
        td = t * diverge
        half = energy - 0.2 * td * energy
        lag_energy = energy - 0.4 * td * half
        lag_density = d_s[l] * inverse(1.0 + td)
        lm[l + 2, 0] = lag_density
        lm[l + 2, 1] = lag_density * lag_energy
        nvx = xp[l + 1, 0] - rate * (xp[l + 2, 1] - xp[l, 1])
        nvx_h[l + 1] = nvx
        nvx_out[l] = nvx
        nvy_out[l] = vy - rate * diff_y(xp[l + 1, 1], 1)

    @pl.loop(0, 4)
    def _(i):
        lagrange(i + (i // 2) * (layers - 4))

    second = [
        remote(lm.at[pl.ds(2, 2)], lm.at[pl.ds(layers + 2, 2)], 4, x_prev),
        remote(lm.at[pl.ds(layers, 2)], lm.at[pl.ds(0, 2)], 5, x_next),
        remote(nvx_h.at[1], nvx_h.at[layers + 1], 6, x_prev),
        remote(nvx_h.at[layers], nvx_h.at[0], 7, x_next),
    ]
    for copy in second:
        copy.start()

    @pl.loop(2, layers - 2)
    def _(l):
        lagrange(l)

    def sweep_x(lower, upper):
        @pl.loop(0, rows // 8)
        def _(block):
            part = pl.ds(pl.multiple_of(block * 8, 8), 8)

            def slope(f, l):
                return limited(f[l] - f[l - 1], f[l + 1] - f[l])

            courants = {}
            for l in range(lower - 1, upper):
                courant = (0.5 * t) * (nvx_h[l + 1, part] + nvx_h[l + 2, part])
                courants[l] = (courant,) + upwind(courant)
            for field in range(2):
                f = {l: lm[l + 2, field, part] for l in range(lower - 2, upper + 2)}
                here = slope(f, lower - 1)
                flux = None
                for l in range(lower - 1, upper):
                    courant, positive, weight = courants[l]
                    after = slope(f, l + 1)
                    face = jnp.where(positive, f[l], f[l + 1]) + weight * jnp.where(positive, here, after)
                    now = courant * face
                    if flux is not None:
                        swept[l, field, part] = f[l] + flux - now
                    flux, here = now, after

    def pack(buffer, parts):
        for side, edge in enumerate((0, rows - 2)):
            for first_row, part in parts:
                to = pl.ds(first_row, part.stop - part.start)
                for j in range(2):
                    for field in range(2):
                        buffer[side, 2 * field + j, to] = swept[part, field, edge + j, :]
                buffer[side, 4, to] = nvy_out[part, 0 if side == 0 else rows - 1, :]

    def send_rows(buffer, low, high, index):
        copies = [
            remote(buffer.at[0], high, index, y_prev),
            remote(buffer.at[1], low, index + 1, y_next),
        ]
        for copy in copies:
            copy.start()
        return copies

    sweep_x(2, layers - 2)
    pack(m_send, [(0, slice(2, layers - 2))])
    middle = send_rows(m_send, m_lo, m_hi, 8)
    for copy in second:
        copy.wait()
    sweep_x(0, 2)
    sweep_x(layers - 2, layers)
    pack(o_send, [(0, slice(0, 2)), (2, slice(layers - 2, layers))])
    outer = send_rows(o_send, o_lo, o_hi, 10)
    for copy in middle:
        copy.wait()

    tile = lax.broadcasted_iota(jnp.int32, (8, cols), 0)

    def sweep(fields, velocity, axis):
        size = velocity.shape[axis]

        def ahead(f):
            return pltpu.roll(f, size - 1, axis)

        def behind(f):
            return pltpu.roll(f, 1, axis)

        courant = (0.5 * t) * (velocity + ahead(velocity))
        positive, weight = upwind(courant)
        out = []
        for f in fields:
            after = ahead(f)
            right = after - f
            slope = limited(behind(right), right)
            face = jnp.where(positive, f, after) + weight * jnp.where(positive, slope, ahead(slope))
            flux = courant * face
            out.append(f + behind(flux) - flux)
        return out

    def finish(l, place, c_lo, c_hi, top):
        def halo(low_first, low_last, high_first, high_last):
            low = jnp.where(tile == 7, c_lo[low_last, pl.ds(place, 1), :], c_lo[low_first, pl.ds(place, 1), :])
            high = jnp.where(tile == 0, c_hi[high_first, pl.ds(place, 1), :], c_hi[high_last, pl.ds(place, 1), :])
            return jnp.where(tile < 4, high, low)

        fields = [
            jnp.concatenate([swept[l, k], halo(2 * k, 2 * k + 1, 2 * k, 2 * k + 1)], axis=0)
            for k in range(2)
        ]
        nvy = nvy_out[l]
        velocity = jnp.concatenate([nvy, halo(4, 4, 4, 4)], axis=0)
        fields = [f[:rows] for f in sweep(fields, velocity, 0)]
        nvz = nvz_out[l]
        density, mass = sweep(fields, nvz, 1)
        energy = mass * inverse(density)
        dens_out[l] = density
        energy_out[l] = energy
        speed = jnp.sqrt(0.56 * energy) + jnp.abs(nvx_out[l]) + jnp.abs(nvy) + jnp.abs(nvz)
        return jnp.maximum(top, speed)

    top = lax.fori_loop(
        0, layers - 4, lambda i, top: finish(i + 2, i, m_lo, m_hi, top), jnp.zeros((rows, cols), jnp.float32)
    )
    for copy in outer:
        copy.wait()
    top = lax.fori_loop(
        0, 4, lambda i, top: finish(i + (i // 2) * (layers - 4), i, o_lo, o_hi, top), top
    )

    def reduced(value):
        return jnp.full((8, 128), jnp.max(value), jnp.float32)

    def share(value, slot, buffer, count, device, sends, recvs):
        top_s[slot] = value
        copies = [
            pltpu.make_async_remote_copy(
                src_ref=top_s.at[slot], dst_ref=buffer.at[step - 1],
                send_sem=sends.at[step - 1], recv_sem=recvs.at[step - 1],
                device_id=device(step), device_id_type=MESH,
            )
            for step in range(1, count)
        ]
        for copy in copies:
            copy.start()
        for copy in copies:
            copy.wait()
        for step in range(1, count):
            value = jnp.maximum(value, buffer[step - 1])
        return value

    best = share(reduced(top), 0, top_x, nx, along_x, x_send, x_recv)
    best = share(best, 1, top_y, ny, along_y, y_send, y_recv)
    limit_out[0] = jnp.max(0.5 / best)


def local(nx, ny, density, energy, velocity_x, velocity_y, velocity_z, time_step):
    layers, rows, cols = density.shape
    full = jax.ShapeDtypeStruct(density.shape, jnp.float32)

    def vmem(*shape):
        return pltpu.VMEM(shape, jnp.float32)

    dma = pltpu.SemaphoreType.DMA
    results = pl.pallas_call(
        functools.partial(kernel, nx, ny),
        out_shape=(full,) * 5 + (jax.ShapeDtypeStruct((1,), jnp.float32),),
        in_specs=[pl.BlockSpec(memory_space=pltpu.SMEM)] + [pl.BlockSpec(memory_space=pltpu.HBM)] * 5,
        out_specs=(pl.BlockSpec(memory_space=pltpu.VMEM),) * 5 + (pl.BlockSpec(memory_space=pltpu.SMEM),),
        scratch_shapes=[
            vmem(layers, rows, cols), vmem(layers, rows, cols),
            vmem(layers + 2, 2, rows, cols),
            vmem(layers, rows, cols), vmem(layers, rows, cols),
            vmem(layers, rows, cols), vmem(layers, rows, cols),
            vmem(2, 2, layers, cols), vmem(2, layers, cols), vmem(2, layers, cols),
            vmem(layers + 4, 2, rows, cols),
            vmem(layers + 2, rows, cols),
            vmem(layers, 2, rows, cols),
            vmem(2, 5, layers - 4, cols), vmem(5, layers - 4, cols), vmem(5, layers - 4, cols),
            vmem(2, 5, 4, cols), vmem(5, 4, cols), vmem(5, 4, cols),
            vmem(2, 8, 128), vmem(nx - 1, 8, 128), vmem(ny - 1, 8, 128),
            dma((5,)), dma((12,)), dma((12,)),
            dma((nx - 1,)), dma((nx - 1,)), dma((ny - 1,)), dma((ny - 1,)),
        ],
        compiler_params=pltpu.CompilerParams(
            collective_id=0, has_side_effects=True, vmem_limit_bytes=32 * 1024 * 1024
        ),
    )(time_step, *(pltpu.with_memory_space_constraint(f, pltpu.HBM) for f in (density, energy, velocity_x, velocity_y, velocity_z)))
    stored = pl.pallas_call(
        store,
        out_shape=(full,) * 5,
        in_specs=[pl.BlockSpec(memory_space=pl.ANY)] * 5,
        out_specs=(pl.BlockSpec(memory_space=pltpu.HBM),) * 5,
        scratch_shapes=[dma((5,))],
    )(*results[:5])
    return (*stored, results[5])


def solution(mesh):
    block = P("gx", "gy", None)
    return jax.shard_map(
        functools.partial(local, mesh.shape["gx"], mesh.shape["gy"]),
        mesh=mesh,
        in_specs=(block,) * 5 + (P(),),
        out_specs=(block,) * 5 + (P(),),
        check_vma=False,
    )
```

```python
import functools

import jax
import jax.numpy as jnp
from jax import lax
from jax.experimental import pallas as pl
from jax.experimental.pallas import tpu as pltpu
from jax.sharding import PartitionSpec as P

MESH = pl.DeviceIdType.MESH


def inverse(value):
    guess = pl.reciprocal(value, approx=True)
    return guess * (2.0 - value * guess)


def limited(left, right):
    product = left * right
    return jnp.maximum(product, 0.0) * inverse(jnp.where(product > 0, left + right, 1.0))


def upwind(courant):
    positive = courant > 0
    return positive, jnp.where(positive, 1.0, -1.0) - courant


def store(*refs):
    sources, targets, sem = refs[:5], refs[5:10], refs[10]
    layers = sources[0].shape[0]
    middle = layers // 2
    parts = (pl.ds(0, middle), pl.ds(middle, layers - middle))
    copies = [
        pltpu.make_async_copy(source.at[part], target.at[part], sem.at[k, side])
        for k, (source, target) in enumerate(zip(sources, targets))
        for side, part in enumerate(parts)
    ]
    for copy in copies:
        copy.start()
    for copy in copies:
        copy.wait()


def kernel(
    nx, ny,
    t_ref, d_hbm, e_hbm, vx_hbm, vy_hbm, vz_hbm,
    dens_out, energy_out, nvx_out, nvy_out, nvz_out, limit_out,
    d_s, e_s, xp, vy_s, vz_s, div_s, rate_s,
    a_send, a_lo, a_hi, lm, nvx_h, swept, m_send, m_lo, m_hi, o_send, o_lo, o_hi,
    top_s, top_x, top_y,
    load_sem, send_sem, recv_sem, x_send, x_recv, y_send, y_recv,
):
    layers, rows, cols = d_s.shape
    ix, iy = lax.axis_index("gx"), lax.axis_index("gy")

    def along_x(step):
        return (lax.rem(ix + step, nx), iy)

    def along_y(step):
        return (ix, lax.rem(iy + step, ny))

    barrier = pltpu.get_barrier_semaphore()
    for step in range(1, nx):
        pl.semaphore_signal(barrier, inc=1, device_id=along_x(step), device_id_type=MESH)
    for step in range(1, ny):
        pl.semaphore_signal(barrier, inc=1, device_id=along_y(step), device_id_type=MESH)

    loads = [
        pltpu.make_async_copy(d_hbm, d_s, load_sem.at[0]),
        pltpu.make_async_copy(e_hbm, e_s, load_sem.at[1]),
        pltpu.make_async_copy(vx_hbm, xp.at[pl.ds(1, layers), 0], load_sem.at[2]),
        pltpu.make_async_copy(vy_hbm, vy_s, load_sem.at[3]),
        pltpu.make_async_copy(vz_hbm, vz_s, load_sem.at[4]),
    ]
    for load in loads:
        load.start()
    t = t_ref[0]

    def remote(src, dst, index, device):
        return pltpu.make_async_remote_copy(
            src_ref=src, dst_ref=dst, send_sem=send_sem.at[index], recv_sem=recv_sem.at[index],
            device_id=device, device_id_type=MESH,
        )

    x_next, x_prev = along_x(1), along_x(nx - 1)
    y_next, y_prev = along_y(1), along_y(ny - 1)

    for load in loads[:2]:
        load.wait()

    @pl.loop(0, layers)
    def _(l):
        xp[l + 1, 1] = 0.4 * d_s[l] * e_s[l]

    for load in loads[2:4]:
        load.wait()
    a_send[0, 0] = vy_s[:, 0, :]
    a_send[0, 1] = xp[1 : layers + 1, 1, 0, :]
    a_send[1, 0] = vy_s[:, rows - 1, :]
    a_send[1, 1] = xp[1 : layers + 1, 1, rows - 1, :]

    pl.semaphore_wait(barrier, nx - 1 + ny - 1)
    first = [
        remote(xp.at[1], xp.at[layers + 1], 0, x_prev),
        remote(xp.at[layers], xp.at[0], 1, x_next),
        remote(a_send.at[0], a_hi, 2, y_prev),
        remote(a_send.at[1], a_lo, 3, y_next),
    ]
    for copy in first:
        copy.start()
    loads[4].wait()

    @pl.loop(0, layers)
    def _(l):
        rate = (0.5 * t) * inverse(d_s[l])
        vz, p = vz_s[l], xp[l + 1, 1]
        rate_s[l] = rate
        div_s[l] = 0.5 * (pltpu.roll(vz, cols - 1, 1) - pltpu.roll(vz, 1, 1))
        nvz_out[l] = vz - rate * (pltpu.roll(p, cols - 1, 1) - pltpu.roll(p, 1, 1))

    for copy in first:
        copy.wait()

    row = lax.broadcasted_iota(jnp.int32, (rows, cols), 0)

    def lagrange(l):
        def diff_y(f, which):
            ahead = jnp.where(row == rows - 1, a_hi[which, pl.ds(l, 1), :], pltpu.roll(f, rows - 1, 0))
            behind = jnp.where(row == 0, a_lo[which, pl.ds(l, 1), :], pltpu.roll(f, 1, 0))
            return ahead - behind

        rate, vy, energy = rate_s[l], vy_s[l], e_s[l]
        diverge = 0.5 * (xp[l + 2, 0] - xp[l, 0]) + 0.5 * diff_y(vy, 0) + div_s[l]
        td = t * diverge
        half = energy - 0.2 * td * energy
        lag_energy = energy - 0.4 * td * half
        lag_density = d_s[l] * inverse(1.0 + td)
        lm[l + 2, 0] = lag_density
        lm[l + 2, 1] = lag_density * lag_energy
        nvx = xp[l + 1, 0] - rate * (xp[l + 2, 1] - xp[l, 1])
        nvx_h[l + 1] = nvx
        nvx_out[l] = nvx
        nvy_out[l] = vy - rate * diff_y(xp[l + 1, 1], 1)

    @pl.loop(0, 4)
    def _(i):
        lagrange(i + (i // 2) * (layers - 4))

    second = [
        remote(lm.at[pl.ds(2, 2)], lm.at[pl.ds(layers + 2, 2)], 4, x_prev),
        remote(lm.at[pl.ds(layers, 2)], lm.at[pl.ds(0, 2)], 5, x_next),
        remote(nvx_h.at[1], nvx_h.at[layers + 1], 6, x_prev),
        remote(nvx_h.at[layers], nvx_h.at[0], 7, x_next),
    ]
    for copy in second:
        copy.start()

    @pl.loop(2, layers - 2)
    def _(l):
        lagrange(l)

    def sweep_x(lower, upper):
        @pl.loop(0, rows // 8)
        def _(block):
            part = pl.ds(pl.multiple_of(block * 8, 8), 8)

            def slope(f, l):
                return limited(f[l] - f[l - 1], f[l + 1] - f[l])

            courants = {}
            for l in range(lower - 1, upper):
                courant = (0.5 * t) * (nvx_h[l + 1, part] + nvx_h[l + 2, part])
                courants[l] = (courant,) + upwind(courant)
            for field in range(2):
                f = {l: lm[l + 2, field, part] for l in range(lower - 2, upper + 2)}
                here = slope(f, lower - 1)
                flux = None
                for l in range(lower - 1, upper):
                    courant, positive, weight = courants[l]
                    after = slope(f, l + 1)
                    face = jnp.where(positive, f[l], f[l + 1]) + weight * jnp.where(positive, here, after)
                    now = courant * face
                    if flux is not None:
                        swept[l, field, part] = f[l] + flux - now
                    flux, here = now, after

    def pack(buffer, parts):
        for side, edge in enumerate((0, rows - 2)):
            for first_row, part in parts:
                to = pl.ds(first_row, part.stop - part.start)
                for j in range(2):
                    for field in range(2):
                        buffer[side, 2 * field + j, to] = swept[part, field, edge + j, :]
                buffer[side, 4, to] = nvy_out[part, 0 if side == 0 else rows - 1, :]

    def send_rows(buffer, low, high, index):
        copies = [
            remote(buffer.at[0], high, index, y_prev),
            remote(buffer.at[1], low, index + 1, y_next),
        ]
        for copy in copies:
            copy.start()
        return copies

    sweep_x(2, layers - 2)
    pack(m_send, [(0, slice(2, layers - 2))])
    middle = send_rows(m_send, m_lo, m_hi, 8)
    for copy in second:
        copy.wait()
    sweep_x(0, 2)
    sweep_x(layers - 2, layers)
    pack(o_send, [(0, slice(0, 2)), (2, slice(layers - 2, layers))])
    outer = send_rows(o_send, o_lo, o_hi, 10)
    for copy in middle:
        copy.wait()

    tile = lax.broadcasted_iota(jnp.int32, (8, cols), 0)

    def sweep(fields, velocity, axis):
        size = velocity.shape[axis]

        def ahead(f):
            return pltpu.roll(f, size - 1, axis)

        def behind(f):
            return pltpu.roll(f, 1, axis)

        courant = (0.5 * t) * (velocity + ahead(velocity))
        positive, weight = upwind(courant)
        out = []
        for f in fields:
            after = ahead(f)
            right = after - f
            slope = limited(behind(right), right)
            face = jnp.where(positive, f, after) + weight * jnp.where(positive, slope, ahead(slope))
            flux = courant * face
            out.append(f + behind(flux) - flux)
        return out

    def finish(l, place, c_lo, c_hi, top):
        def halo(low_first, low_last, high_first, high_last):
            low = jnp.where(tile == 7, c_lo[low_last, pl.ds(place, 1), :], c_lo[low_first, pl.ds(place, 1), :])
            high = jnp.where(tile == 0, c_hi[high_first, pl.ds(place, 1), :], c_hi[high_last, pl.ds(place, 1), :])
            return jnp.where(tile < 4, high, low)

        fields = [
            jnp.concatenate([swept[l, k], halo(2 * k, 2 * k + 1, 2 * k, 2 * k + 1)], axis=0)
            for k in range(2)
        ]
        nvy = nvy_out[l]
        velocity = jnp.concatenate([nvy, halo(4, 4, 4, 4)], axis=0)
        fields = [f[:rows] for f in sweep(fields, velocity, 0)]
        nvz = nvz_out[l]
        density, mass = sweep(fields, nvz, 1)
        energy = mass * inverse(density)
        dens_out[l] = density
        energy_out[l] = energy
        speed = jnp.sqrt(0.56 * energy) + jnp.abs(nvx_out[l]) + jnp.abs(nvy) + jnp.abs(nvz)
        return jnp.maximum(top, speed)

    top = lax.fori_loop(
        0, layers - 4, lambda i, top: finish(i + 2, i, m_lo, m_hi, top), jnp.zeros((rows, cols), jnp.float32)
    )
    for copy in outer:
        copy.wait()
    top = lax.fori_loop(
        0, 4, lambda i, top: finish(i + (i // 2) * (layers - 4), i, o_lo, o_hi, top), top
    )

    def reduced(value):
        return jnp.full((8, 128), jnp.max(value), jnp.float32)

    def share(value, slot, buffer, count, device, sends, recvs):
        top_s[slot] = value
        copies = [
            pltpu.make_async_remote_copy(
                src_ref=top_s.at[slot], dst_ref=buffer.at[step - 1],
                send_sem=sends.at[step - 1], recv_sem=recvs.at[step - 1],
                device_id=device(step), device_id_type=MESH,
            )
            for step in range(1, count)
        ]
        for copy in copies:
            copy.start()
        for copy in copies:
            copy.wait()
        for step in range(1, count):
            value = jnp.maximum(value, buffer[step - 1])
        return value

    best = share(reduced(top), 0, top_x, nx, along_x, x_send, x_recv)
    best = share(best, 1, top_y, ny, along_y, y_send, y_recv)
    limit_out[0] = jnp.max(0.5 / best)


def local(nx, ny, density, energy, velocity_x, velocity_y, velocity_z, time_step):
    layers, rows, cols = density.shape
    full = jax.ShapeDtypeStruct(density.shape, jnp.float32)

    def vmem(*shape):
        return pltpu.VMEM(shape, jnp.float32)

    dma = pltpu.SemaphoreType.DMA
    results = pl.pallas_call(
        functools.partial(kernel, nx, ny),
        out_shape=(full,) * 5 + (jax.ShapeDtypeStruct((1,), jnp.float32),),
        in_specs=[pl.BlockSpec(memory_space=pltpu.SMEM)] + [pl.BlockSpec(memory_space=pltpu.HBM)] * 5,
        out_specs=(pl.BlockSpec(memory_space=pltpu.VMEM),) * 5 + (pl.BlockSpec(memory_space=pltpu.SMEM),),
        scratch_shapes=[
            vmem(layers, rows, cols), vmem(layers, rows, cols),
            vmem(layers + 2, 2, rows, cols),
            vmem(layers, rows, cols), vmem(layers, rows, cols),
            vmem(layers, rows, cols), vmem(layers, rows, cols),
            vmem(2, 2, layers, cols), vmem(2, layers, cols), vmem(2, layers, cols),
            vmem(layers + 4, 2, rows, cols),
            vmem(layers + 2, rows, cols),
            vmem(layers, 2, rows, cols),
            vmem(2, 5, layers - 4, cols), vmem(5, layers - 4, cols), vmem(5, layers - 4, cols),
            vmem(2, 5, 4, cols), vmem(5, 4, cols), vmem(5, 4, cols),
            vmem(2, 8, 128), vmem(nx - 1, 8, 128), vmem(ny - 1, 8, 128),
            dma((5,)), dma((12,)), dma((12,)),
            dma((nx - 1,)), dma((nx - 1,)), dma((ny - 1,)), dma((ny - 1,)),
        ],
        compiler_params=pltpu.CompilerParams(
            collective_id=0, has_side_effects=True, vmem_limit_bytes=32 * 1024 * 1024
        ),
    )(time_step, *(pltpu.with_memory_space_constraint(f, pltpu.HBM) for f in (density, energy, velocity_x, velocity_y, velocity_z)))
    stored = pl.pallas_call(
        store,
        out_shape=(full,) * 5,
        in_specs=[pl.BlockSpec(memory_space=pltpu.VMEM)] * 5,
        out_specs=(pl.BlockSpec(memory_space=pltpu.HBM),) * 5,
        scratch_shapes=[dma((5, 2))],
    )(*results[:5])
    return (*stored, results[5])


def solution(mesh):
    block = P("gx", "gy", None)
    return jax.shard_map(
        functools.partial(local, mesh.shape["gx"], mesh.shape["gy"]),
        mesh=mesh,
        in_specs=(block,) * 5 + (P(),),
        out_specs=(block,) * 5 + (P(),),
        check_vma=False,
    )
```

```python
import functools

import jax
import jax.numpy as jnp
from jax import lax
from jax.experimental import pallas as pl
from jax.experimental.pallas import tpu as pltpu
from jax.sharding import PartitionSpec as P

MESH = pl.DeviceIdType.MESH


def inverse(value):
    guess = pl.reciprocal(value, approx=True)
    return guess * (2.0 - value * guess)


def limited(left, right):
    product = left * right
    return jnp.maximum(product, 0.0) * inverse(jnp.where(product > 0, left + right, 1.0))


def upwind(courant):
    positive = courant > 0
    return positive, jnp.where(positive, 1.0, -1.0) - courant


def store(*refs):
    sources, targets, held, load_sem, store_sem = refs[:5], refs[5:10], refs[10], refs[11], refs[12]
    layers = sources[0].shape[0]
    middle = layers // 2
    parts = (pl.ds(0, middle), pl.ds(middle, layers - middle))
    loads, stores = [], []
    for k, (source, target) in enumerate(zip(sources, targets)):
        for side, part in enumerate(parts):
            loads.append(pltpu.make_async_copy(source.at[part], held.at[k, part], load_sem.at[k, side]))
            stores.append(pltpu.make_async_copy(held.at[k, part], target.at[part], store_sem.at[k, side]))
    for copy in loads:
        copy.start()
    for load, copy in zip(loads, stores):
        load.wait()
        copy.start()
    for copy in stores:
        copy.wait()


def kernel(
    nx, ny,
    t_ref, d_hbm, e_hbm, vx_hbm, vy_hbm, vz_hbm,
    dens_hbm, energy_hbm, nvx_hbm, nvy_hbm, nvz_hbm, limit_out,
    dens_out, energy_out, nvx_out, nvy_out, nvz_out,
    d_s, e_s, xp, vy_s, vz_s, div_s, rate_s,
    a_send, a_lo, a_hi, lm, nvx_h, swept, m_send, m_lo, m_hi, o_send, o_lo, o_hi,
    top_s, top_x, top_y,
    load_sem, out_sem, send_sem, recv_sem, x_send, x_recv, y_send, y_recv,
):
    layers, rows, cols = d_s.shape
    ix, iy = lax.axis_index("gx"), lax.axis_index("gy")

    def along_x(step):
        return (lax.rem(ix + step, nx), iy)

    def along_y(step):
        return (ix, lax.rem(iy + step, ny))

    barrier = pltpu.get_barrier_semaphore()
    for step in range(1, nx):
        pl.semaphore_signal(barrier, inc=1, device_id=along_x(step), device_id_type=MESH)
    for step in range(1, ny):
        pl.semaphore_signal(barrier, inc=1, device_id=along_y(step), device_id_type=MESH)

    loads = [
        pltpu.make_async_copy(d_hbm, d_s, load_sem.at[0]),
        pltpu.make_async_copy(e_hbm, e_s, load_sem.at[1]),
        pltpu.make_async_copy(vx_hbm, xp.at[pl.ds(1, layers), 0], load_sem.at[2]),
        pltpu.make_async_copy(vy_hbm, vy_s, load_sem.at[3]),
        pltpu.make_async_copy(vz_hbm, vz_s, load_sem.at[4]),
    ]
    for load in loads:
        load.start()
    t = t_ref[0]

    def remote(src, dst, index, device):
        return pltpu.make_async_remote_copy(
            src_ref=src, dst_ref=dst, send_sem=send_sem.at[index], recv_sem=recv_sem.at[index],
            device_id=device, device_id_type=MESH,
        )

    x_next, x_prev = along_x(1), along_x(nx - 1)
    y_next, y_prev = along_y(1), along_y(ny - 1)

    for load in loads[:2]:
        load.wait()

    @pl.loop(0, layers)
    def _(l):
        xp[l + 1, 1] = 0.4 * d_s[l] * e_s[l]

    for load in loads[2:4]:
        load.wait()
    a_send[0, 0] = vy_s[:, 0, :]
    a_send[0, 1] = xp[1 : layers + 1, 1, 0, :]
    a_send[1, 0] = vy_s[:, rows - 1, :]
    a_send[1, 1] = xp[1 : layers + 1, 1, rows - 1, :]

    pl.semaphore_wait(barrier, nx - 1 + ny - 1)
    first = [
        remote(xp.at[1], xp.at[layers + 1], 0, x_prev),
        remote(xp.at[layers], xp.at[0], 1, x_next),
        remote(a_send.at[0], a_hi, 2, y_prev),
        remote(a_send.at[1], a_lo, 3, y_next),
    ]
    for copy in first:
        copy.start()
    loads[4].wait()

    @pl.loop(0, layers)
    def _(l):
        rate = (0.5 * t) * inverse(d_s[l])
        vz, p = vz_s[l], xp[l + 1, 1]
        rate_s[l] = rate
        div_s[l] = 0.5 * (pltpu.roll(vz, cols - 1, 1) - pltpu.roll(vz, 1, 1))
        nvz_out[l] = vz - rate * (pltpu.roll(p, cols - 1, 1) - pltpu.roll(p, 1, 1))

    for copy in first:
        copy.wait()

    row = lax.broadcasted_iota(jnp.int32, (rows, cols), 0)

    def lagrange(l):
        def diff_y(f, which):
            ahead = jnp.where(row == rows - 1, a_hi[which, pl.ds(l, 1), :], pltpu.roll(f, rows - 1, 0))
            behind = jnp.where(row == 0, a_lo[which, pl.ds(l, 1), :], pltpu.roll(f, 1, 0))
            return ahead - behind

        rate, vy, energy = rate_s[l], vy_s[l], e_s[l]
        diverge = 0.5 * (xp[l + 2, 0] - xp[l, 0]) + 0.5 * diff_y(vy, 0) + div_s[l]
        td = t * diverge
        half = energy - 0.2 * td * energy
        lag_energy = energy - 0.4 * td * half
        lag_density = d_s[l] * inverse(1.0 + td)
        lm[l + 2, 0] = lag_density
        lm[l + 2, 1] = lag_density * lag_energy
        nvx = xp[l + 1, 0] - rate * (xp[l + 2, 1] - xp[l, 1])
        nvx_h[l + 1] = nvx
        nvx_out[l] = nvx
        nvy_out[l] = vy - rate * diff_y(xp[l + 1, 1], 1)

    @pl.loop(0, 4)
    def _(i):
        lagrange(i + (i // 2) * (layers - 4))

    second = [
        remote(lm.at[pl.ds(2, 2)], lm.at[pl.ds(layers + 2, 2)], 4, x_prev),
        remote(lm.at[pl.ds(layers, 2)], lm.at[pl.ds(0, 2)], 5, x_next),
        remote(nvx_h.at[1], nvx_h.at[layers + 1], 6, x_prev),
        remote(nvx_h.at[layers], nvx_h.at[0], 7, x_next),
    ]
    for copy in second:
        copy.start()

    @pl.loop(2, layers - 2)
    def _(l):
        lagrange(l)

    stores = []

    def store_part(source, target, part=slice(None)):
        copy = pltpu.make_async_copy(source.at[part], target.at[part], out_sem.at[len(stores)])
        copy.start()
        stores.append(copy)

    store_part(nvx_out, nvx_hbm)
    store_part(nvy_out, nvy_hbm)
    store_part(nvz_out, nvz_hbm)

    def sweep_x(lower, upper):
        @pl.loop(0, rows // 8)
        def _(block):
            part = pl.ds(pl.multiple_of(block * 8, 8), 8)

            def slope(f, l):
                return limited(f[l] - f[l - 1], f[l + 1] - f[l])

            courants = {}
            for l in range(lower - 1, upper):
                courant = (0.5 * t) * (nvx_h[l + 1, part] + nvx_h[l + 2, part])
                courants[l] = (courant,) + upwind(courant)
            for field in range(2):
                f = {l: lm[l + 2, field, part] for l in range(lower - 2, upper + 2)}
                here = slope(f, lower - 1)
                flux = None
                for l in range(lower - 1, upper):
                    courant, positive, weight = courants[l]
                    after = slope(f, l + 1)
                    face = jnp.where(positive, f[l], f[l + 1]) + weight * jnp.where(positive, here, after)
                    now = courant * face
                    if flux is not None:
                        swept[l, field, part] = f[l] + flux - now
                    flux, here = now, after

    def pack(buffer, parts):
        for side, edge in enumerate((0, rows - 2)):
            for first_row, part in parts:
                to = pl.ds(first_row, part.stop - part.start)
                for j in range(2):
                    for field in range(2):
                        buffer[side, 2 * field + j, to] = swept[part, field, edge + j, :]
                buffer[side, 4, to] = nvy_out[part, 0 if side == 0 else rows - 1, :]

    def send_rows(buffer, low, high, index):
        copies = [
            remote(buffer.at[0], high, index, y_prev),
            remote(buffer.at[1], low, index + 1, y_next),
        ]
        for copy in copies:
            copy.start()
        return copies

    sweep_x(2, layers - 2)
    pack(m_send, [(0, slice(2, layers - 2))])
    middle = send_rows(m_send, m_lo, m_hi, 8)
    for copy in second:
        copy.wait()
    sweep_x(0, 2)
    sweep_x(layers - 2, layers)
    pack(o_send, [(0, slice(0, 2)), (2, slice(layers - 2, layers))])
    outer = send_rows(o_send, o_lo, o_hi, 10)
    for copy in middle:
        copy.wait()

    tile = lax.broadcasted_iota(jnp.int32, (8, cols), 0)

    def sweep(fields, velocity, axis):
        size = velocity.shape[axis]

        def ahead(f):
            return pltpu.roll(f, size - 1, axis)

        def behind(f):
            return pltpu.roll(f, 1, axis)

        courant = (0.5 * t) * (velocity + ahead(velocity))
        positive, weight = upwind(courant)
        out = []
        for f in fields:
            after = ahead(f)
            right = after - f
            slope = limited(behind(right), right)
            face = jnp.where(positive, f, after) + weight * jnp.where(positive, slope, ahead(slope))
            flux = courant * face
            out.append(f + behind(flux) - flux)
        return out

    def finish(l, place, c_lo, c_hi, top):
        def halo(low_first, low_last, high_first, high_last):
            low = jnp.where(tile == 7, c_lo[low_last, pl.ds(place, 1), :], c_lo[low_first, pl.ds(place, 1), :])
            high = jnp.where(tile == 0, c_hi[high_first, pl.ds(place, 1), :], c_hi[high_last, pl.ds(place, 1), :])
            return jnp.where(tile < 4, high, low)

        fields = [
            jnp.concatenate([swept[l, k], halo(2 * k, 2 * k + 1, 2 * k, 2 * k + 1)], axis=0)
            for k in range(2)
        ]
        nvy = nvy_out[l]
        velocity = jnp.concatenate([nvy, halo(4, 4, 4, 4)], axis=0)
        fields = [f[:rows] for f in sweep(fields, velocity, 0)]
        nvz = nvz_out[l]
        density, mass = sweep(fields, nvz, 1)
        energy = mass * inverse(density)
        dens_out[l] = density
        energy_out[l] = energy
        speed = jnp.sqrt(0.56 * energy) + jnp.abs(nvx_out[l]) + jnp.abs(nvy) + jnp.abs(nvz)
        return jnp.maximum(top, speed)

    top = lax.fori_loop(
        0, layers - 4, lambda i, top: finish(i + 2, i, m_lo, m_hi, top), jnp.zeros((rows, cols), jnp.float32)
    )
    store_part(dens_out, dens_hbm, pl.ds(2, layers - 4))
    store_part(energy_out, energy_hbm, pl.ds(2, layers - 4))
    for copy in outer:
        copy.wait()
    top = lax.fori_loop(
        0, 4, lambda i, top: finish(i + (i // 2) * (layers - 4), i, o_lo, o_hi, top), top
    )

    for part in (pl.ds(0, 2), pl.ds(layers - 2, 2)):
        store_part(dens_out, dens_hbm, part)
        store_part(energy_out, energy_hbm, part)

    def reduced(value):
        return jnp.full((8, 128), jnp.max(value), jnp.float32)

    def share(value, slot, buffer, count, device, sends, recvs):
        top_s[slot] = value
        copies = [
            pltpu.make_async_remote_copy(
                src_ref=top_s.at[slot], dst_ref=buffer.at[step - 1],
                send_sem=sends.at[step - 1], recv_sem=recvs.at[step - 1],
                device_id=device(step), device_id_type=MESH,
            )
            for step in range(1, count)
        ]
        for copy in copies:
            copy.start()
        for copy in copies:
            copy.wait()
        for step in range(1, count):
            value = jnp.maximum(value, buffer[step - 1])
        return value

    best = share(reduced(top), 0, top_x, nx, along_x, x_send, x_recv)
    best = share(best, 1, top_y, ny, along_y, y_send, y_recv)
    limit_out[0] = jnp.max(0.5 / best)
    for copy in stores:
        copy.wait()


def local(nx, ny, density, energy, velocity_x, velocity_y, velocity_z, time_step):
    layers, rows, cols = density.shape
    full = jax.ShapeDtypeStruct(density.shape, jnp.float32)

    def vmem(*shape):
        return pltpu.VMEM(shape, jnp.float32)

    dma = pltpu.SemaphoreType.DMA
    results = pl.pallas_call(
        functools.partial(kernel, nx, ny),
        out_shape=(pltpu.HBM(density.shape, jnp.float32),) * 5 + (jax.ShapeDtypeStruct((1,), jnp.float32),),
        in_specs=[pl.BlockSpec(memory_space=pltpu.SMEM)] + [pl.BlockSpec(memory_space=pltpu.HBM)] * 5,
        out_specs=(pl.BlockSpec(memory_space=pltpu.HBM),) * 5 + (pl.BlockSpec(memory_space=pltpu.SMEM),),
        scratch_shapes=[
            *(vmem(layers, rows, cols) for _ in range(5)),
            vmem(layers, rows, cols), vmem(layers, rows, cols),
            vmem(layers + 2, 2, rows, cols),
            vmem(layers, rows, cols), vmem(layers, rows, cols),
            vmem(layers, rows, cols), vmem(layers, rows, cols),
            vmem(2, 2, layers, cols), vmem(2, layers, cols), vmem(2, layers, cols),
            vmem(layers + 4, 2, rows, cols),
            vmem(layers + 2, rows, cols),
            vmem(layers, 2, rows, cols),
            vmem(2, 5, layers - 4, cols), vmem(5, layers - 4, cols), vmem(5, layers - 4, cols),
            vmem(2, 5, 4, cols), vmem(5, 4, cols), vmem(5, 4, cols),
            vmem(2, 8, 128), vmem(nx - 1, 8, 128), vmem(ny - 1, 8, 128),
            dma((5,)), dma((9,)), dma((12,)), dma((12,)),
            dma((nx - 1,)), dma((nx - 1,)), dma((ny - 1,)), dma((ny - 1,)),
        ],
        compiler_params=pltpu.CompilerParams(
            collective_id=0, has_side_effects=True, vmem_limit_bytes=32 * 1024 * 1024
        ),
    )(time_step, *(pltpu.with_memory_space_constraint(f, pltpu.HBM) for f in (density, energy, velocity_x, velocity_y, velocity_z)))
    stored = pl.pallas_call(
        store,
        out_shape=(full,) * 5,
        in_specs=[pl.BlockSpec(memory_space=pltpu.HBM)] * 5,
        out_specs=(pl.BlockSpec(memory_space=pltpu.HBM),) * 5,
        scratch_shapes=[vmem(5, layers, rows, cols), dma((5, 2)), dma((5, 2))],
    )(*(pltpu.with_memory_space_constraint(f, pltpu.HBM) for f in results[:5]))
    return (*stored, results[5])


def solution(mesh):
    block = P("gx", "gy", None)
    return jax.shard_map(
        functools.partial(local, mesh.shape["gx"], mesh.shape["gy"]),
        mesh=mesh,
        in_specs=(block,) * 5 + (P(),),
        out_specs=(block,) * 5 + (P(),),
        check_vma=False,
    )
```
